256 devices in a mesh: section: 8 (over y, x_lo), lat: 32 (over x_hi, z, core).
Axes of the slice: x: 4 (x_hi: 2, x_lo: 2; x = x_hi * 2 + x_lo), y: 4, z: 8, core: 2. Of those that a mesh axis runs over, the one named last changes fastest.
Arguments:
- stacked: bfloat16 [1024, 16384], P('lat', 'section'), may hold values from -6 to 6
- enc_weight: bfloat16 [16384, 16384], P('section', 'lat'), may hold values from -0.046875 to 0.046875
- enc_bias: float32 [16384], P('lat'), may hold values from -3 to 3
- dec_weight: bfloat16 [16384, 16384], P('lat', 'section'), may hold values from -0.046875 to 0.046875
- dec_bias: float32 [16384], P('section'), may hold values from -3 to 3
- active: int32 [1024, 16384], P(None, 'lat'), may hold values 0 or 1
- upstream: bfloat16 [1024, 16384], P('lat', 'section'), may hold values from -0.3984375 to 0.3984375
Outputs:
- rebuilt: bfloat16 [1024, 16384], P('lat', 'section')
- enc_grad: bfloat16 [16384, 16384], P('section', 'lat')
- dec_grad: bfloat16 [16384, 16384], P('lat', 'section')
The draws below stay inside these ranges and needn't reach their ends.
All inputs are finite; a program needn't handle non-finite values. No bound on the sum of `active` on one device may be relied on, other than what follows from the above.
Results may differ from the reference program's by a relative error of at most 0.0049.
Values may be sent and summed in bfloat16 or wider, within the bound.
A program may use at most 128 MiB of HBM per device.

```python
import jax
import jax.numpy as jnp
from jax import lax

LATENTS = 16384
TOKENS = 1024
LD = 16384


def with_ends(drawn, stream_key, low, largest):
    index_at = [jax.random.randint(jax.random.fold_in(stream_key, axis), (), 0, length) for axis, length in enumerate(drawn.shape)]
    main_axis = drawn.shape.index(max(drawn.shape))
    next_to = index_at[:main_axis] + [(index_at[main_axis] + 1) % drawn.shape[main_axis]] + index_at[main_axis + 1:]
    return drawn.at[tuple(index_at)].set(low).at[tuple(next_to)].set(largest)


def shard_levels(rng, extent, shards, smallest, high):
    level, own = 1.0, jax.random.fold_in(rng, 6)
    for axis_at, parts in shards:
        draws = jnp.exp(jax.random.uniform(jax.random.fold_in(own, axis_at), (parts,), jnp.float32, smallest / len(shards), high / len(shards)))
        level = level * jnp.repeat(draws, extent[axis_at] // parts).reshape([-1 if axis == axis_at else 1 for axis in range(len(extent))])
    return level


def normal_values(rng, extent, deviation, limit, shards=(), held_as=jnp.bfloat16):
    level = shard_levels(rng, extent, shards, -0.22, 0.18) if shards else 1.0
    values = jax.random.normal(rng, extent, jnp.float32) * deviation * level
    return jnp.minimum(jnp.maximum(values, -limit), limit).astype(held_as)


def setup_inputs(seed: int = 0) -> dict:
    seeds = jax.random.split(jax.random.key(seed), 8)
    return {
        "stacked": normal_values(seeds[0], (TOKENS, LD), 1.0, 6.0, ((0, 32), (1, 8))),
        "enc_weight": normal_values(seeds[1], (LD, LATENTS), LD ** -0.5, 0.046875, ((0, 8), (1, 32))),
        "enc_bias": normal_values(seeds[2], (LATENTS,), 0.5, 3.0, ((0, 32),), jnp.float32),
        "dec_weight": normal_values(seeds[3], (LATENTS, LD), LATENTS ** -0.5, 0.046875, ((0, 32), (1, 8))),
        "dec_bias": normal_values(seeds[4], (LD,), 0.5, 3.0, ((0, 8),), jnp.float32),
        "active": with_ends((jax.random.randint(seeds[5], (TOKENS, LATENTS), 0, 2) < 1).astype(jnp.int32), jax.random.fold_in(seeds[5], 1), 0, 1),
        "upstream": normal_values(seeds[6], (TOKENS, LD), 0.0625, 0.3984375, ((0, 32), (1, 8))),
    }


def reference(stacked, enc_weight, enc_bias, dec_weight, dec_bias, active, upstream):
    gating = active.astype(jnp.float32)
    preact = jnp.dot(stacked, enc_weight, preferred_element_type=jnp.float32) + enc_bias
    latent = (gating * preact).astype(jnp.bfloat16)
    rebuilt = (jnp.dot(latent, dec_weight, preferred_element_type=jnp.float32) + dec_bias).astype(jnp.bfloat16)
    dec_grad = lax.dot_general(latent, upstream, (((0,), (0,)), ((), ())), preferred_element_type=jnp.float32).astype(jnp.bfloat16)
    latent_grad = lax.dot_general(upstream, dec_weight, (((1,), (1,)), ((), ())), preferred_element_type=jnp.float32)
    pre_grad = (gating * latent_grad).astype(jnp.bfloat16)
    enc_grad = lax.dot_general(stacked, pre_grad, (((0,), (0,)), ((), ())), preferred_element_type=jnp.float32).astype(jnp.bfloat16)
    return rebuilt, enc_grad, dec_grad
```

```python
import jax
import jax.numpy as jnp
from jax import lax
from jax.experimental import pallas as pl
from jax.experimental.pallas import tpu as pltpu
from jax.sharding import PartitionSpec as P

F32, BF16 = jnp.float32, jnp.bfloat16
MESH = pl.DeviceIdType.MESH
B = 32
FEAT = 2048
LATS = 512
TOK = 1024
CH = 256

PLACE = {1: 0, 7: 1, 2: 2, 6: 3, 3: 4, 5: 5, 0: 6, 4: 7}
PAIRS = ((1, 7), (2, 6), (3, 5), (0, 4))


def row(d, core, half):
    return PLACE[d] * 128 + core * 64 + half * 32


GZ = (
    (-1, 0, 0, 1), (1, 0, 0, 7), (-1, 1, 0, 2), (1, 7, 0, 6), (-1, 2, 0, 3), (1, 6, 0, 5),
    (-1, 3, 0, 4), (-1, 2, 1, 3), (1, 6, 1, 5), (1, 5, 1, 4),
)
GZ_INTO = {(there, half): i for i, (_, _, half, there) in enumerate(GZ)}
GX = (0, 1, 7, 2, 6)

RZ = (
    (1, 4, 0, 3), (-1, 4, 1, 5), (1, 3, 1, 2), (-1, 5, 0, 6), (1, 3, 0, 2), (-1, 5, 1, 6),
    (1, 2, 0, 1), (-1, 6, 0, 7), (1, 1, 0, 0), (-1, 7, 0, 0),
)
RZ_OF = {(here, half): i for i, (_, here, half, _) in enumerate(RZ)}


def rz_into(d, half):
    return [i for i, (_, _, h, there) in enumerate(RZ) if (there, h) == (d, half)]


def kernel(
    x_hbm, we_hbm, be_hbm, wd_hbm, bd_hbm, act_hbm, up_hbm,
    reb_hbm, ge_hbm, gd_hbm,
    xs, us, we, wd, be, bd, act,
    part, full, own, yin, xout, xin, lat, pre,
    dec, cin, stage, zin, xrin, ge, gd, reb,
    load_sem, store_sem, gz_s, gz_r, gx_s, gx_r, gc_s, gc_r,
    ry_s, ry_r, rx_s, rx_r, ax_s, ax_r, ay_s, ay_r,
    dc_s, dc_r, rz_s, rz_r, xr_s, xr_r,
):
    s = lax.axis_index("section")
    l = lax.axis_index("lat")
    y, xl = s // 2, lax.rem(s, 2)
    xh, z, c = l // 16, lax.rem(l, 16) // 2, lax.rem(l, 2)

    def at_lat(h, zz, cc):
        return h * 16 + zz * 2 + cc

    zdev = {
        1: (s, at_lat(xh, lax.rem(z + 1, 8), c)),
        -1: (s, at_lat(xh, lax.rem(z + 7, 8), c)),
    }
    xdev = (s, at_lat(1 - xh, z, c))
    cdev = (s, at_lat(xh, z, 1 - c))
    ypos = [lax.rem(y + k, 4) for k in (1, 2, 3)]
    ydev = [(p * 2 + xl, l) for p in ypos]
    sdev = (y * 2 + 1 - xl, l)

    def remote(src, dst, ssem, rsem, dev):
        return pltpu.make_async_remote_copy(
            src_ref=src, dst_ref=dst, send_sem=ssem, recv_sem=rsem, device_id=dev, device_id_type=MESH
        )

    mine = pl.ds(row(0, 0, 0), B)
    loads = [
        pltpu.make_async_copy(x_hbm, xs.at[mine], load_sem.at[0]),
        pltpu.make_async_copy(up_hbm, us.at[mine], load_sem.at[1]),
        pltpu.make_async_copy(we_hbm, we, load_sem.at[2]),
        pltpu.make_async_copy(wd_hbm, wd, load_sem.at[3]),
        pltpu.make_async_copy(be_hbm, be, load_sem.at[4]),
        pltpu.make_async_copy(bd_hbm, bd, load_sem.at[5]),
    ]
    pair, score, shalf = s // 4, lax.rem(s, 4) // 2, lax.rem(s, 2)
    for q, (d0, d1) in enumerate(PAIRS):
        dist = d0 + pair * (d1 - d0)
        owner = at_lat(
            lax.rem(xh + shalf, 2), lax.rem(z + dist, 8), lax.rem(c + score, 2)
        )
        loads.append(
            pltpu.make_async_copy(
                act_hbm.at[pl.ds(pl.multiple_of(owner * B, B), B)], act.at[q], load_sem.at[6 + q]
            )
        )
    for copy in loads:
        copy.start()

    barrier = pltpu.get_barrier_semaphore()
    everyone = [zdev[1], zdev[-1], xdev, cdev, sdev] + ydev
    for dev in everyone:
        pl.semaphore_signal(barrier, inc=1, device_id=dev, device_id_type=MESH)
    pl.semaphore_wait(barrier, len(everyone))

    sent = []

    def start(copy):
        copy.start()
        sent.append(copy)

    def flush():
        for copy in sent:
            copy.wait_send()
        sent.clear()

    tokens = (xs, us)

    def gz(t, i):
        direction, here, half, there = GZ[i]
        return remote(
            tokens[t].at[pl.ds(row(here, 0, half), B)], tokens[t].at[pl.ds(row(there, 0, half), B)],
            gz_s.at[t, i], gz_r.at[t, i], zdev[direction],
        )

    def gx(t, d):
        i = GX.index(d)
        return remote(
            tokens[t].at[pl.ds(row(d, 0, 0), B)], tokens[t].at[pl.ds(row(d, 0, 1), B)],
            gx_s.at[t, i], gx_r.at[t, i], xdev,
        )

    def gc(t, d):
        return remote(
            tokens[t].at[pl.ds(row(d, 0, 0), 2 * B)], tokens[t].at[pl.ds(row(d, 1, 0), 2 * B)],
            gc_s.at[t, d], gc_r.at[t, d], cdev,
        )

    def got_z(t, d, half):
        gz(t, GZ_INTO[d, half]).wait_recv()

    def got_x(t, d):
        gx(t, d).wait_recv()

    def gather(t, step):
        if step == 0:
            loads[t].wait()
            start(gz(t, 0))
            start(gz(t, 1))
            start(gx(t, 0))
        elif step == 1:
            got_z(t, 1, 0)
            start(gz(t, 2))
            start(gx(t, 1))
            got_z(t, 7, 0)
            start(gz(t, 3))
            start(gx(t, 7))
            got_x(t, 0)
            start(gc(t, 0))
        elif step == 2:
            got_z(t, 2, 0)
            start(gz(t, 4))
            start(gx(t, 2))
            got_z(t, 6, 0)
            start(gz(t, 5))
            start(gx(t, 6))
            got_x(t, 1)
            start(gc(t, 1))
            got_x(t, 7)
            start(gc(t, 7))
        elif step == 3:
            got_z(t, 3, 0)
            start(gz(t, 6))
            got_x(t, 2)
            start(gz(t, 7))
            start(gc(t, 2))
            got_z(t, 5, 0)
            got_x(t, 6)
            start(gz(t, 8))
            start(gc(t, 6))
        elif step == 4:
            got_z(t, 5, 1)
            start(gz(t, 9))
            start(gc(t, 5))
            got_z(t, 3, 1)
            start(gc(t, 3))
        else:
            got_z(t, 4, 0)
            got_z(t, 4, 1)
            start(gc(t, 4))

    result = (lat, pre)

    def ry(t, q, k):
        return remote(
            part.at[t, pl.ds(pl.multiple_of(q * CH + ypos[k] * 64, 64), 64)], yin.at[t, q, k],
            ry_s.at[t, q, k], ry_r.at[t, q, k], ydev[k],
        )

    def rx(t, q):
        return remote(xout.at[t, q], xin.at[t, q], rx_s.at[t, q], rx_r.at[t, q], sdev)

    def ax(t, q):
        rows = pl.ds(pl.multiple_of(q * CH + s * B, B), B)
        return remote(result[t].at[rows], result[t].at[rows], ax_s.at[t, q], ax_r.at[t, q], sdev)

    def ay(t, q, k):
        rows = pl.ds(pl.multiple_of(q * CH + y * 64, 64), 64)
        return remote(result[t].at[rows], result[t].at[rows], ay_s.at[t, q, k], ay_r.at[t, q, k], ydev[k])

    def sec_a(t, q):
        for d in PAIRS[q]:
            gc(t, d).wait_recv()
        rows = pl.ds(q * CH, CH)
        if t == 0:
            acc = jnp.dot(xs[rows], we[...], preferred_element_type=F32)
        else:
            acc = lax.dot_general(us[rows], wd[...], (((1,), (1,)), ((), ())), preferred_element_type=F32)
        full[...] = acc
        part[t, rows] = acc.astype(BF16)
        for k in (1, 0, 2):
            start(ry(t, q, k))
        own[t, q] = full[pl.ds(pl.multiple_of(y * 64, 64), 64)]

    def sec_b(t, q):
        for k in range(3):
            ry(t, q, k).wait_recv()
        own[t, q] = (
            own[t, q] + yin[t, q, 0].astype(F32) + yin[t, q, 1].astype(F32) + yin[t, q, 2].astype(F32)
        )
        xout[t, q] = own[t, q, pl.ds(pl.multiple_of((1 - xl) * B, B), B)]
        start(rx(t, q))

    def sec_c(t, q):
        rx(t, q).wait_recv()
        total = own[t, q, pl.ds(pl.multiple_of(xl * B, B), B)] + xin[t, q]
        if t == 0:
            total = total + be[...]
        value = (act[q].astype(F32) * total).astype(BF16)
        result[t][pl.ds(pl.multiple_of(q * CH + s * B, B), B)] = value
        start(ax(t, q))

    def sec_d(t, q):
        ax(t, q).wait_recv()
        for k in (1, 0, 2):
            start(ay(t, q, k))

    def sec_e(t, q):
        for k in range(3):
            ay(t, q, k).wait_recv()

    def dc(d):
        return remote(dec.at[pl.ds(row(d, 1, 0), 2 * B)], cin.at[d], dc_s.at[d], dc_r.at[d], cdev)

    def decode(q):
        sec_e(0, q)

        @pl.loop(0, 4)
        def _(n):
            cols = pl.ds(pl.multiple_of(n * 512, 512), 512)
            dec[pl.ds(q * CH, CH), cols] = jnp.dot(
                lat[pl.ds(q * CH, CH)], wd[:, cols], preferred_element_type=F32
            )

        for d in PAIRS[q]:
            start(dc(d))

    def rz(i):
        return remote(stage.at[i], zin.at[i], rz_s.at[i], rz_r.at[i], zdev[RZ[i][0]])

    def xr(i):
        return remote(stage.at[10 + i], xrin.at[i], xr_s.at[i], xr_r.at[i], xdev)

    def total(d, half, cols):
        value = dec[pl.ds(row(d, 0, half), B), cols] + cin[d, pl.ds(half * B, B), cols]
        for i in rz_into(d, half):
            value = value + zin[i, :, cols].astype(F32)
        if half == 0 and d in GX:
            value = value + xrin[GX.index(d), :, cols].astype(F32)
        return value

    def arrived(d, half):
        for i in rz_into(d, half):
            rz(i).wait_recv()
        if half == 0 and d in GX:
            xr(GX.index(d)).wait_recv()

    def reduce(d, half):
        arrived(d, half)
        i = RZ_OF.get((d, half))
        slot = 10 + GX.index(d) if i is None else i

        @pl.loop(0, 4)
        def _(n):
            cols = pl.ds(pl.multiple_of(n * 512, 512), 512)
            stage[slot, :, cols] = total(d, half, cols).astype(BF16)

        start(xr(slot - 10) if i is None else rz(i))

    def finish():
        arrived(0, 0)

        @pl.loop(0, 4)
        def _(n):
            cols = pl.ds(pl.multiple_of(n * 512, 512), 512)
            reb[:, cols] = (total(0, 0, cols) + bd[:, cols]).astype(BF16)

        copy = pltpu.make_async_copy(reb, reb_hbm, store_sem.at[0])
        copy.start()
        return copy

    def dec_grad(n):
        cols = pl.ds(n * 512, 512)
        gd[:, cols] = lax.dot_general(
            lat[...], us[:, cols], (((0,), (0,)), ((), ())), preferred_element_type=F32
        ).astype(BF16)

    def enc_grad(n):
        @pl.loop(0, 4)
        def _(m):
            at = n * 1024 + m * 256
            rows = pl.ds(pl.multiple_of(at, 256), 256)
            ge[rows] = lax.dot_general(
                xs[:, rows], pre[...], (((0,), (0,)), ((), ())), preferred_element_type=F32
            ).astype(BF16)

        rows = pl.ds(n * 1024, 1024)
        copy = pltpu.make_async_copy(ge.at[rows], ge_hbm.at[rows], store_sem.at[2 + n])
        copy.start()
        return copy

    gather(0, 0)
    gather(0, 1)
    gather(1, 0)
    gather(0, 2)
    loads[2].wait()
    sec_a(0, 0)
    gather(1, 1)
    gather(0, 3)
    sec_a(0, 1)
    gather(1, 2)
    sec_b(0, 0)
    gather(0, 4)
    sec_a(0, 2)
    for copy in loads[3:]:
        copy.wait()
    gather(1, 3)
    sec_a(1, 0)
    sec_b(0, 1)
    sec_c(0, 0)
    gather(0, 5)
    sec_a(0, 3)
    gather(1, 4)
    sec_a(1, 1)
    sec_b(0, 2)
    sec_c(0, 1)
    sec_d(0, 0)
    sec_b(1, 0)
    gather(1, 5)
    sec_b(0, 3)
    sec_c(0, 2)
    sec_d(0, 1)
    sec_a(1, 2)
    sec_c(0, 3)
    sec_d(0, 2)
    sec_b(1, 1)
    sec_c(1, 0)
    sec_d(0, 3)
    sec_a(1, 3)
    decode(0)
    decode(1)
    sec_b(1, 2)
    sec_c(1, 1)
    sec_d(1, 0)
    decode(2)
    sec_b(1, 3)
    decode(3)
    for d in range(8):
        dc(d).wait_recv()
    for unit in ((4, 0), (4, 1), (3, 1), (5, 0), (1, 1), (7, 1), (0, 1)):
        reduce(*unit)
    sec_c(1, 2)
    sec_d(1, 1)
    sec_c(1, 3)
    reduce(3, 0)
    reduce(5, 1)
    sec_d(1, 2)
    sec_d(1, 3)
    dec_grad(0)
    reduce(2, 1)
    reduce(6, 1)
    dec_grad(1)
    dec_grad(2)
    reduce(2, 0)
    reduce(6, 0)
    dec_grad(3)
    stores = [pltpu.make_async_copy(gd, gd_hbm, store_sem.at[1])]
    stores[0].start()
    for q in range(4):
        sec_e(1, q)
    reduce(1, 0)
    reduce(7, 0)
    stores.append(enc_grad(0))
    stores.append(finish())
    stores.append(enc_grad(1))
    flush()
    for copy in stores:
        copy.wait()


def per_device(stacked, enc_weight, enc_bias, dec_weight, dec_bias, active, upstream):
    hbm = pl.BlockSpec(memory_space=pl.ANY)
    dma = pltpu.SemaphoreType.DMA
    return pl.pallas_call(
        kernel,
        out_shape=(
            jax.ShapeDtypeStruct((B, FEAT), BF16),
            jax.ShapeDtypeStruct((FEAT, LATS), BF16),
            jax.ShapeDtypeStruct((LATS, FEAT), BF16),
        ),
        in_specs=[hbm] * 7,
        out_specs=(hbm,) * 3,
        scratch_shapes=[
            pltpu.VMEM((TOK, FEAT), BF16),
            pltpu.VMEM((TOK, FEAT), BF16),
            pltpu.VMEM((FEAT, LATS), BF16),
            pltpu.VMEM((LATS, FEAT), BF16),
            pltpu.VMEM((1, LATS), F32),
            pltpu.VMEM((1, FEAT), F32),
            pltpu.VMEM((4, B, LATS), jnp.int32),
            pltpu.VMEM((2, TOK, LATS), BF16),
            pltpu.VMEM((CH, LATS), F32),
            pltpu.VMEM((2, 4, 64, LATS), F32),
            pltpu.VMEM((2, 4, 3, 64, LATS), BF16),
            pltpu.VMEM((2, 4, B, LATS), F32),
            pltpu.VMEM((2, 4, B, LATS), F32),
            pltpu.VMEM((TOK, LATS), BF16),
            pltpu.VMEM((TOK, LATS), BF16),
            pltpu.VMEM((TOK, FEAT), F32),
            pltpu.VMEM((8, 2 * B, FEAT), F32),
            pltpu.VMEM((15, B, FEAT), BF16),
            pltpu.VMEM((10, B, FEAT), BF16),
            pltpu.VMEM((5, B, FEAT), BF16),
            pltpu.VMEM((FEAT, LATS), BF16),
            pltpu.VMEM((LATS, FEAT), BF16),
            pltpu.VMEM((B, FEAT), BF16),
            dma((10,)), dma((4,)),
            dma((2, 10)), dma((2, 10)), dma((2, 5)), dma((2, 5)), dma((2, 8)), dma((2, 8)),
            dma((2, 4, 3)), dma((2, 4, 3)), dma((2, 4)), dma((2, 4)),
            dma((2, 4)), dma((2, 4)), dma((2, 4, 3)), dma((2, 4, 3)),
            dma((8,)), dma((8,)), dma((10,)), dma((10,)), dma((5,)), dma((5,)),
        ],
        compiler_params=pltpu.CompilerParams(
            collective_id=0, has_side_effects=True, vmem_limit_bytes=58 << 20
        ),
        cost_estimate=pl.CostEstimate(flops=10 * 1024 * 2048 * 512, bytes_accessed=14 << 20, transcendentals=0),
    )(
        stacked, enc_weight, enc_bias.reshape(1, -1), dec_weight, dec_bias.reshape(1, -1), active, upstream
    )


def solution(mesh):
    placed = (
        P("lat", "section"),
        P("section", "lat"),
        P("lat"),
        P("lat", "section"),
        P("section"),
        P(None, "lat"),
        P("lat", "section"),
    )
    return jax.shard_map(
        per_device,
        mesh=mesh,
        in_specs=placed,
        out_specs=(P("lat", "section"), P("section", "lat"), P("lat", "section")),
        check_vma=False,
    )
```

```python
import jax
import jax.numpy as jnp
from jax import lax
from jax.experimental import pallas as pl
from jax.experimental.pallas import tpu as pltpu
from jax.sharding import PartitionSpec as P

F32, BF16 = jnp.float32, jnp.bfloat16
MESH = pl.DeviceIdType.MESH
B = 32
H = 16
FEAT = 2048
LATS = 512
TOK = 1024
CH = 256

PLACE = {1: 0, 7: 1, 2: 2, 6: 3, 3: 4, 5: 5, 0: 6, 4: 7}
PAIRS = ((1, 7), (2, 6), (3, 5), (0, 4))


def row(a, d, core, half):
    group, place = divmod(PLACE[d], 4)
    return a * 512 + group * CH + core * 128 + place * 32 + half * H


SPREAD_X = (
    (None, "z", -1, (0, 0), (1, 0)), (None, "z", 1, (0, 0), (7, 0)), (None, "x", 0, (0, 0), (0, 1)),
    (None, "z", -1, (1, 0), (2, 0)), (None, "z", 1, (7, 0), (6, 0)), (None, "x", 0, (1, 0), (1, 1)),
    (None, "x", 0, (7, 0), (7, 1)), (None, "z", -1, (2, 0), (3, 0)), (None, "z", 1, (6, 0), (5, 0)),
    (None, "x", 0, (2, 0), (2, 1)), (None, "x", 0, (6, 0), (6, 1)), (0, "z", -1, (3, 0), (4, 0)),
    (1, "z", 1, (5, 0), (4, 0)), (None, "z", -1, (2, 1), (3, 1)), (None, "z", 1, (6, 1), (5, 1)),
    (None, "x", 0, (4, 0), (4, 1)),
)
SPREAD_UP = (
    (None, "z", -1, (0, 0), (1, 0)), (None, "z", 1, (0, 0), (7, 0)), (None, "x", 0, (0, 0), (0, 1)),
    (None, "z", -1, (1, 0), (2, 0)), (None, "z", 1, (7, 0), (6, 0)), (None, "x", 0, (1, 0), (1, 1)),
    (None, "x", 0, (7, 0), (7, 1)), (None, "z", -1, (2, 0), (3, 0)), (None, "z", 1, (6, 0), (5, 0)),
    (None, "z", -1, (1, 1), (2, 1)), (None, "z", 1, (7, 1), (6, 1)), (0, "z", -1, (3, 0), (4, 0)),
    (1, "z", 1, (5, 0), (4, 0)), (None, "z", -1, (2, 1), (3, 1)), (None, "z", 1, (6, 1), (5, 1)),
    (0, "z", 1, (5, 1), (4, 1)), (1, "z", -1, (3, 1), (4, 1)),
)
SPREAD = (SPREAD_X, SPREAD_UP)
SUM = (
    (1, "z", 2, (4, 1), (2, 1)), (0, "z", -2, (4, 1), (6, 1)), (None, "z", -1, (5, 1), (6, 1)),
    (None, "z", 1, (3, 1), (2, 1)), (None, "x", 0, (7, 1), (7, 0)), (None, "x", 0, (1, 1), (1, 0)),
    (None, "z", -1, (5, 0), (6, 0)), (None, "z", 1, (3, 0), (2, 0)), (None, "x", 0, (6, 1), (6, 0)),
    (None, "x", 0, (2, 1), (2, 0)), (1, "z", -2, (4, 0), (6, 0)), (0, "z", 2, (4, 0), (2, 0)),
    (None, "x", 0, (0, 1), (0, 0)), (None, "z", -1, (7, 0), (0, 0)), (None, "z", 1, (1, 0), (0, 0)),
    (None, "z", -2, (6, 0), (0, 0)), (None, "z", 2, (2, 0), (0, 0)),
)

def leaving(table, a, block):
    return [i for i, (part, _, _, here, _) in enumerate(table) if part in (None, a) and here == block]


def coming(table, a, block):
    return [i for i, (part, _, _, _, there) in enumerate(table) if part in (None, a) and there == block]


PLAN = (
    ("take", 0, 0, 0, 0), ("take", 0, 1, 0, 0), ("take", 0, 0, 1, 0), ("take", 0, 0, 7, 0), ("ready", 4, 5),
    ("ready", 5, 8), ("take", 0, 0, 0, 1), ("ready", 8, 24), ("take", 0, 1, 1, 0), ("take", 0, 1, 7, 0),
    ("take", 0, 1, 0, 1), ("take", 0, 0, 2, 0), ("take", 0, 0, 6, 0), ("take", 0, 0, 1, 1),
    ("take", 0, 1, 2, 0), ("take", 0, 1, 6, 0), ("take", 0, 0, 7, 1), ("share", 0, 0, 0),
    ("take", 0, 1, 1, 1), ("take", 0, 0, 3, 0), ("take", 0, 0, 5, 0), ("take", 0, 1, 7, 1),
    ("share", 0, 1, 0), ("take", 0, 1, 3, 0), ("take", 0, 1, 5, 0), ("take", 0, 0, 2, 1),
    ("take", 0, 0, 4, 0), ("take", 0, 0, 6, 1), ("share", 0, 0, 1), ("take", 0, 1, 4, 0),
    ("take", 0, 1, 2, 1), ("take", 1, 0, 0, 0), ("sec_a", 0, 0), ("take", 0, 0, 3, 1), ("take", 0, 1, 6, 1),
    ("share", 0, 1, 1), ("take", 1, 1, 0, 0), ("take", 0, 0, 5, 1), ("share", 0, 0, 2), ("take", 0, 0, 4, 1),
    ("share", 0, 0, 3), ("sec_a", 0, 2), ("take", 0, 1, 3, 1), ("take", 0, 1, 4, 1), ("share", 0, 1, 3),
    ("take", 1, 0, 7, 0), ("sec_a", 0, 1), ("take", 0, 1, 5, 1), ("share", 0, 1, 2), ("take", 1, 0, 0, 1),
    ("take", 1, 0, 1, 0), ("take", 1, 1, 1, 0), ("sec_b", 0, 0), ("take", 1, 1, 0, 1), ("take", 1, 1, 7, 0),
    ("sec_a", 0, 3), ("take", 1, 0, 6, 0), ("take", 1, 0, 7, 1), ("sec_b", 0, 2), ("take", 1, 0, 2, 0),
    ("take", 1, 0, 1, 1), ("share", 1, 0, 0), ("take", 1, 1, 6, 0), ("take", 1, 1, 2, 0),
    ("take", 1, 1, 1, 1), ("sec_b", 0, 1), ("take", 1, 0, 5, 0), ("sec_c", 0, 0), ("take", 1, 0, 3, 0),
    ("take", 1, 0, 6, 1), ("take", 1, 1, 7, 1), ("share", 1, 1, 0), ("sec_c", 0, 2), ("sec_b", 0, 3),
    ("take", 1, 0, 2, 1), ("take", 1, 1, 5, 0), ("share", 1, 0, 1), ("sec_c", 0, 1), ("take", 1, 1, 3, 0),
    ("take", 1, 0, 5, 1), ("sec_a", 1, 0), ("decode", 0), ("sec_c", 0, 3), ("take", 1, 0, 4, 0),
    ("take", 1, 1, 2, 1), ("take", 1, 1, 6, 1), ("take", 1, 1, 4, 0), ("share", 1, 1, 1),
    ("take", 1, 0, 3, 1), ("share", 1, 0, 2), ("decode", 2), ("collect", 0, 0), ("reduce", 0, 1, 1),
    ("reduce", 0, 7, 1), ("take", 1, 0, 4, 1), ("share", 1, 0, 3), ("collect", 0, 1), ("decode", 1),
    ("take", 1, 1, 3, 1), ("take", 1, 1, 5, 1), ("sec_a", 1, 2), ("collect", 2, 0), ("reduce", 1, 1, 1),
    ("reduce", 1, 7, 1), ("share", 1, 1, 2), ("reduce", 0, 1, 0), ("sec_b", 1, 0), ("collect", 2, 1),
    ("sec_a", 1, 1), ("reduce", 0, 7, 0), ("take", 1, 1, 4, 1), ("share", 1, 1, 3), ("collect", 1, 0),
    ("reduce", 0, 3, 1), ("reduce", 0, 5, 1), ("reduce", 0, 3, 0), ("reduce", 0, 5, 0), ("decode", 3),
    ("reduce", 1, 1, 0), ("collect", 1, 1), ("reduce", 0, 4, 1), ("reduce", 0, 4, 0), ("reduce", 0, 0, 1),
    ("sec_a", 1, 3), ("reduce", 1, 7, 0), ("reduce", 0, 2, 1), ("sec_c", 1, 0), ("collect", 3, 0),
    ("reduce", 1, 3, 1), ("reduce", 1, 5, 1), ("reduce", 1, 3, 0), ("reduce", 1, 5, 0), ("sec_b", 1, 2),
    ("collect", 3, 1), ("reduce", 1, 4, 1), ("reduce", 1, 4, 0), ("reduce", 1, 0, 1), ("sec_b", 1, 1),
    ("dec_grad", 0), ("dec_grad", 1), ("reduce", 0, 6, 1), ("reduce", 0, 2, 0), ("sec_b", 1, 3),
    ("sec_c", 1, 2), ("dec_grad", 2), ("dec_grad", 3), ("sec_c", 1, 1), ("reduce", 1, 6, 1), ("sec_e", 1, 0),
    ("reduce", 0, 6, 0), ("sec_c", 1, 3), ("reduce", 1, 2, 1), ("sec_e", 1, 2), ("reduce", 1, 6, 0),
    ("sec_e", 1, 1), ("finish", 0), ("reduce", 1, 2, 0), ("sec_e", 1, 3), ("enc_grad", 0), ("enc_grad", 1),
    ("enc_grad", 2), ("finish", 1), ("enc_grad", 3),
)

def kernel(
    x_hbm, we_hbm, be_hbm, wd_hbm, bd_hbm, act_hbm, up_hbm,
    reb_hbm, ge_hbm, gd_hbm,
    xs, us, we, wd, be, bd, act,
    part, full, own, yin, xout, xin, lat, pre,
    dec, cin, stage, sums_in, ge, gd, reb,
    load_sem, store_sem, g_s, g_r, gc_s, gc_r,
    ry_s, ry_r, rx_s, rx_r, ay_s, ay_r, dc_s, dc_r, s_s, s_r,
):
    s = lax.axis_index("section")
    l = lax.axis_index("lat")
    y, xl = s // 2, lax.rem(s, 2)
    xh, z, c = l // 16, lax.rem(l, 16) // 2, lax.rem(l, 2)

    def at_lat(h, zz, cc):
        return h * 16 + zz * 2 + cc

    zdev = {step: (s, at_lat(xh, lax.rem(z + step + 8, 8), c)) for step in (-2, -1, 1, 2)}
    xdev = (s, at_lat(1 - xh, z, c))
    cdev = (s, at_lat(xh, z, 1 - c))
    ypos = [lax.rem(y + k, 4) for k in (1, 2, 3)]
    ydev = [(p * 2 + xl, l) for p in ypos]
    sdev = (y * 2 + 1 - xl, l)

    def remote(src, dst, sems, at, dev):
        return pltpu.make_async_remote_copy(
            src_ref=src, dst_ref=dst, send_sem=sems[0].at[at], recv_sem=sems[1].at[at], device_id=dev,
            device_id_type=MESH,
        )

    loads = [
        pltpu.make_async_copy(hbm.at[pl.ds(a * H, H)], ref.at[pl.ds(row(a, 0, 0, 0), H)], load_sem.at[t, a])
        for t, (hbm, ref) in enumerate(((x_hbm, xs), (up_hbm, us)))
        for a in (0, 1)
    ]
    loads += [
        pltpu.make_async_copy(we_hbm, we, load_sem.at[2, 0]),
        pltpu.make_async_copy(wd_hbm, wd, load_sem.at[2, 1]),
        pltpu.make_async_copy(be_hbm, be, load_sem.at[3, 0]),
        pltpu.make_async_copy(bd_hbm, bd, load_sem.at[3, 1]),
    ]
    score, other = y // 2, lax.rem(y, 2)
    for q in range(4):
        a, group = divmod(q, 2)
        for n in range(4):
            odd, half = divmod(n, 2)
            dist = (1 - other) * (3 - 6 * odd) + other * 4 * odd if group else (other + 1) * (1 - 2 * odd)
            owner = at_lat(lax.rem(xh + half, 2), lax.rem(z + dist + 8, 8), lax.rem(c + score, 2))
            loads.append(
                pltpu.make_async_copy(
                    act_hbm.at[pl.ds(pl.multiple_of(owner * B + a * H, H), H)],
                    act.at[q, pl.ds(n * H, H)], load_sem.at[4 + q, n],
                )
            )
    for copy in loads:
        copy.start()

    barrier = pltpu.get_barrier_semaphore()
    everyone = list(zdev.values()) + [xdev, cdev, sdev] + ydev
    for dev in everyone:
        pl.semaphore_signal(barrier, inc=1, device_id=dev, device_id_type=MESH)
    pl.semaphore_wait(barrier, len(everyone))

    sent = []

    def start(copy):
        copy.start()
        sent.append(copy)

    stores = []

    def store(copy):
        copy.start()
        stores.append(copy)

    def flush():
        for copy in sent:
            copy.wait_send()
        sent.clear()

    tokens = (xs, us)

    def spread(t, a, i):
        _, axis, step, here, there = SPREAD[t][i]
        return remote(
            tokens[t].at[pl.ds(row(a, here[0], 0, here[1]), H)], tokens[t].at[pl.ds(row(a, there[0], 0, there[1]), H)],
            (g_s, g_r), (t, a, i), xdev if axis == "x" else zdev[step],
        )

    def gc(t, a, p):
        d = PAIRS[p][0]
        return remote(
            tokens[t].at[pl.ds(row(a, d, 0, 0), 4 * H)], tokens[t].at[pl.ds(row(a, d, 1, 0), 4 * H)],
            (gc_s, gc_r), (t, a, p), cdev,
        )

    def take(t, a, d, half):
        if (d, half) == (0, 0):
            loads[2 * t + a].wait()
        for i in coming(SPREAD[t], a, (d, half)):
            spread(t, a, i).wait_recv()
        for i in leaving(SPREAD[t], a, (d, half)):
            start(spread(t, a, i))

    def share(t, a, p):
        start(gc(t, a, p))

    result = (lat, pre)

    def ry(t, q, k):
        return remote(
            part.at[t, pl.ds(pl.multiple_of(q * CH + ypos[k] * 64, 64), 64)], yin.at[t, q, k],
            (ry_s, ry_r), (t, q, k,), ydev[k],
        )

    def rx(t, q):
        return remote(xout.at[t, q], xin.at[t, q], (rx_s, rx_r), (t, q), sdev)

    def ay(t, q, k):
        rows = pl.ds(pl.multiple_of(q * CH + y * 64, 64), 64)
        return remote(result[t].at[rows], result[t].at[rows], (ay_s, ay_r), (t, q, k,), ydev[k])

    def sec_a(t, q):
        a, group = divmod(q, 2)
        gc(t, a, 2 * group).wait_recv()
        gc(t, a, 2 * group + 1).wait_recv()
        rows = pl.ds(q * CH, CH)
        if t == 0:
            acc = jnp.dot(xs[rows], we[...], preferred_element_type=F32)
        else:
            acc = lax.dot_general(us[rows], wd[...], (((1,), (1,)), ((), ())), preferred_element_type=F32)
        full[...] = acc
        part[t, rows] = acc.astype(BF16)
        for k in (1, 0, 2):
            start(ry(t, q, k))
        own[t, q] = full[pl.ds(pl.multiple_of(y * 64, 64), 64)]

    def sec_b(t, q):
        for k in range(3):
            ry(t, q, k).wait_recv()
        own[t, q] = (
            own[t, q] + yin[t, q, 0].astype(F32) + yin[t, q, 1].astype(F32) + yin[t, q, 2].astype(F32)
        )
        xout[t, q] = own[t, q].astype(BF16)
        start(rx(t, q))

    def sec_c(t, q):
        rx(t, q).wait_recv()
        total = own[t, q] + xin[t, q].astype(F32)
        if t == 0:
            total = total + be[...]
        value = (act[q].astype(F32) * total).astype(BF16)
        result[t][pl.ds(pl.multiple_of(q * CH + y * 64, 64), 64)] = value
        for k in (1, 0, 2):
            start(ay(t, q, k))

    def sec_e(t, q):
        for k in range(3):
            ay(t, q, k).wait_recv()

    def dc(q, p):
        rows = pl.ds(q * CH + 128 + p * 64, 64)
        return remote(dec.at[rows], cin.at[q, pl.ds(p * 64, 64)], (dc_s, dc_r), (q, p), cdev)

    def decode(q):
        sec_e(0, q)

        @pl.loop(0, 4)
        def _(n):
            cols = pl.ds(pl.multiple_of(n * 512, 512), 512)
            dec[pl.ds(q * CH, CH), cols] = jnp.dot(
                lat[pl.ds(q * CH, CH)], wd[:, cols], preferred_element_type=F32
            )

        start(dc(q, 0))
        start(dc(q, 1))

    def summed(a, i):
        _, axis, step, _, _ = SUM[i]
        return remote(
            stage.at[a, i], sums_in.at[a, i], (s_s, s_r), (a, i), xdev if axis == "x" else zdev[step]
        )

    def total(a, d, half, cols):
        group, place = divmod(PLACE[d], 4)
        value = dec[pl.ds(row(a, d, 0, half), H), cols] + cin[2 * a + group, pl.ds(place * 32 + half * H, H), cols]
        for i in coming(SUM, a, (d, half)):
            value = value + sums_in[a, i, :, cols].astype(F32)
        return value

    def collect(q, p):
        dc(q, p).wait_recv()

    def arrived(a, d, half):
        for i in coming(SUM, a, (d, half)):
            summed(a, i).wait_recv()

    def reduce(a, d, half):
        arrived(a, d, half)
        (i,) = leaving(SUM, a, (d, half))

        @pl.loop(0, 2)
        def _(n):
            cols = pl.ds(pl.multiple_of(n * 1024, 1024), 1024)
            stage[a, i, :, cols] = total(a, d, half, cols).astype(BF16)

        start(summed(a, i))

    def finish(a):
        arrived(a, 0, 0)
        rows = pl.ds(a * H, H)

        @pl.loop(0, 2)
        def _(n):
            cols = pl.ds(pl.multiple_of(n * 1024, 1024), 1024)
            reb[rows, cols] = (total(a, 0, 0, cols) + bd[:, cols]).astype(BF16)

        store(pltpu.make_async_copy(reb.at[rows], reb_hbm.at[rows], store_sem.at[a]))

    def dec_grad(n):
        cols = pl.ds(n * 512, 512)
        gd[:, cols] = lax.dot_general(
            lat[...], us[:, cols], (((0,), (0,)), ((), ())), preferred_element_type=F32
        ).astype(BF16)
        if n == 3:
            store(pltpu.make_async_copy(gd, gd_hbm, store_sem.at[2]))

    def enc_grad(n):
        for m in (0, 1):
            rows = pl.ds(n * 512 + m * 256, 256)
            ge[rows] = lax.dot_general(
                xs[:, rows], pre[...], (((0,), (0,)), ((), ())), preferred_element_type=F32
            ).astype(BF16)
        rows = pl.ds(n * 512, 512)
        store(pltpu.make_async_copy(ge.at[rows], ge_hbm.at[rows], store_sem.at[3 + n]))

    def ready(first, last):
        for i in range(first, last):
            loads[i].wait()

    phases = {
        f.__name__: f
        for f in (
            ready, take, share, sec_a, sec_b, sec_c, sec_e, decode, collect, reduce, finish, dec_grad, enc_grad
        )
    }
    plan = [(phases[name], args) for name, *args in PLAN]
    for phase, args in plan:
        phase(*args)
    flush()
    for copy in stores:
        copy.wait()


def copy_out(reb, ge, gd, reb_out, ge_out, gd_out, reb_v, ge_v, gd_v, sems):
    pieces = [(reb, reb_v, reb_out, pl.ds(0, B))]
    for src, held, dst in ((ge, ge_v, ge_out), (gd, gd_v, gd_out)):
        step = src.shape[0] // 4
        pieces += [(src, held, dst, pl.ds(n * step, step)) for n in range(4)]
    ins = [
        pltpu.make_async_copy(src.at[rows], held.at[rows], sems.at[0, n])
        for n, (src, held, _, rows) in enumerate(pieces)
    ]
    outs = [
        pltpu.make_async_copy(held.at[rows], dst.at[rows], sems.at[1, n])
        for n, (_, held, dst, rows) in enumerate(pieces)
    ]
    for copy in ins:
        copy.start()
    for arriving, leaving in zip(ins, outs):
        arriving.wait()
        leaving.start()
    for copy in outs:
        copy.wait()


def per_device(stacked, enc_weight, enc_bias, dec_weight, dec_bias, active, upstream):
    hbm = pl.BlockSpec(memory_space=pl.ANY)
    dma = pltpu.SemaphoreType.DMA
    shapes = (
        jax.ShapeDtypeStruct((B, FEAT), BF16),
        jax.ShapeDtypeStruct((FEAT, LATS), BF16),
        jax.ShapeDtypeStruct((LATS, FEAT), BF16),
    )
    outs = pl.pallas_call(
        kernel,
        out_shape=shapes,
        in_specs=[hbm] * 7,
        out_specs=(hbm,) * 3,
        scratch_shapes=[
            pltpu.VMEM((TOK, FEAT), BF16),
            pltpu.VMEM((TOK, FEAT), BF16),
            pltpu.VMEM((FEAT, LATS), BF16),
            pltpu.VMEM((LATS, FEAT), BF16),
            pltpu.VMEM((1, LATS), F32),
            pltpu.VMEM((1, FEAT), F32),
            pltpu.VMEM((4, 64, LATS), jnp.int32),
            pltpu.VMEM((2, TOK, LATS), BF16),
            pltpu.VMEM((CH, LATS), F32),
            pltpu.VMEM((2, 4, 64, LATS), F32),
            pltpu.VMEM((2, 4, 3, 64, LATS), BF16),
            pltpu.VMEM((2, 4, 64, LATS), BF16),
            pltpu.VMEM((2, 4, 64, LATS), BF16),
            pltpu.VMEM((TOK, LATS), BF16),
            pltpu.VMEM((TOK, LATS), BF16),
            pltpu.VMEM((TOK, FEAT), F32),
            pltpu.VMEM((4, 128, FEAT), F32),
            pltpu.VMEM((2, len(SUM), H, FEAT), BF16),
            pltpu.VMEM((2, len(SUM), H, FEAT), BF16),
            pltpu.VMEM((FEAT, LATS), BF16),
            pltpu.VMEM((LATS, FEAT), BF16),
            pltpu.VMEM((B, FEAT), BF16),
            dma((8, 4)), dma((7,)),
            dma((2, 2, max(map(len, SPREAD)))), dma((2, 2, max(map(len, SPREAD)))), dma((2, 2, 4)), dma((2, 2, 4)),
            dma((2, 4, 3)), dma((2, 4, 3)), dma((2, 4)), dma((2, 4)), dma((2, 4, 3)), dma((2, 4, 3)),
            dma((4, 2)), dma((4, 2)), dma((2, len(SUM))), dma((2, len(SUM))),
        ],
        compiler_params=pltpu.CompilerParams(
            collective_id=0, has_side_effects=True, vmem_limit_bytes=58 << 20
        ),
        cost_estimate=pl.CostEstimate(flops=10 * 1024 * 2048 * 512, bytes_accessed=14 << 20, transcendentals=0),
    )(
        stacked, enc_weight, enc_bias.reshape(1, -1), dec_weight, dec_bias.reshape(1, -1), active, upstream
    )
    return pl.pallas_call(
        copy_out,
        out_shape=shapes,
        in_specs=[hbm] * 3,
        out_specs=(hbm,) * 3,
        scratch_shapes=[
            pltpu.VMEM((B, FEAT), BF16),
            pltpu.VMEM((FEAT, LATS), BF16),
            pltpu.VMEM((LATS, FEAT), BF16),
            dma((2, 9)),
        ],
        compiler_params=pltpu.CompilerParams(vmem_limit_bytes=58 << 20),
        cost_estimate=pl.CostEstimate(flops=0, bytes_accessed=9 << 20, transcendentals=0),
    )(*outs)


def solution(mesh):
    placed = (
        P("lat", "section"),
        P("section", "lat"),
        P("lat"),
        P("lat", "section"),
        P("section"),
        P(None, "lat"),
        P("lat", "section"),
    )
    return jax.shard_map(
        per_device,
        mesh=mesh,
        in_specs=placed,
        out_specs=(P("lat", "section"), P("section", "lat"), P("lat", "section")),
        check_vma=False,
    )
```

```python
import jax
import jax.numpy as jnp
from jax import lax
from jax.experimental import pallas as pl
from jax.experimental.pallas import tpu as pltpu
from jax.sharding import PartitionSpec as P

F32, BF16 = jnp.float32, jnp.bfloat16
MESH = pl.DeviceIdType.MESH
B = 32
H = 16
FEAT = 2048
LATS = 512
TOK = 1024
CH = 256

PLACE = {1: 0, 7: 1, 2: 2, 6: 3, 3: 4, 5: 5, 0: 6, 4: 7}
PAIRS = ((1, 7), (2, 6), (3, 5), (0, 4))


def row(a, d, core, half):
    group, place = divmod(PLACE[d], 4)
    return a * 512 + group * CH + core * 128 + place * 32 + half * H


SPREAD_X = (
    (None, "z", -1, (0, 0), (1, 0)), (None, "z", 1, (0, 0), (7, 0)), (None, "x", 0, (0, 0), (0, 1)),
    (None, "z", -1, (1, 0), (2, 0)), (None, "z", 1, (7, 0), (6, 0)), (None, "x", 0, (1, 0), (1, 1)),
    (None, "x", 0, (7, 0), (7, 1)), (None, "z", -1, (2, 0), (3, 0)), (None, "z", 1, (6, 0), (5, 0)),
    (None, "x", 0, (2, 0), (2, 1)), (None, "x", 0, (6, 0), (6, 1)), (0, "z", -1, (3, 0), (4, 0)),
    (1, "z", 1, (5, 0), (4, 0)), (None, "z", -1, (2, 1), (3, 1)), (None, "z", 1, (6, 1), (5, 1)),
    (None, "x", 0, (4, 0), (4, 1)),
)
SPREAD_UP = (
    (None, "z", -1, (0, 0), (1, 0)), (None, "z", 1, (0, 0), (7, 0)), (None, "x", 0, (0, 0), (0, 1)),
    (None, "z", -1, (1, 0), (2, 0)), (None, "z", 1, (7, 0), (6, 0)), (None, "x", 0, (1, 0), (1, 1)),
    (None, "x", 0, (7, 0), (7, 1)), (None, "z", -1, (2, 0), (3, 0)), (None, "z", 1, (6, 0), (5, 0)),
    (None, "z", -1, (1, 1), (2, 1)), (None, "z", 1, (7, 1), (6, 1)), (0, "z", -1, (3, 0), (4, 0)),
    (1, "z", 1, (5, 0), (4, 0)), (None, "z", -1, (2, 1), (3, 1)), (None, "z", 1, (6, 1), (5, 1)),
    (0, "z", 1, (5, 1), (4, 1)), (1, "z", -1, (3, 1), (4, 1)),
)
SPREAD = (SPREAD_X, SPREAD_UP)
SUM = (
    (1, "z", 1, (4, 1), (3, 1)), (0, "z", -1, (4, 1), (5, 1)), (None, "z", -1, (5, 1), (6, 1)),
    (None, "z", 1, (3, 1), (2, 1)), (None, "x", 0, (7, 1), (7, 0)), (None, "x", 0, (1, 1), (1, 0)),
    (1, "z", -1, (4, 0), (5, 0)), (0, "z", 1, (4, 0), (3, 0)), (None, "z", -1, (5, 0), (6, 0)),
    (None, "z", 1, (3, 0), (2, 0)), (None, "x", 0, (6, 1), (6, 0)), (None, "x", 0, (2, 1), (2, 0)),
    (None, "x", 0, (0, 1), (0, 0)), (None, "z", -1, (7, 0), (0, 0)), (None, "z", 1, (1, 0), (0, 0)),
    (None, "z", -2, (6, 0), (0, 0)), (None, "z", 2, (2, 0), (0, 0)),
)

def leaving(table, a, block):
    return [i for i, (part, _, _, here, _) in enumerate(table) if part in (None, a) and here == block]


def coming(table, a, block):
    return [i for i, (part, _, _, _, there) in enumerate(table) if part in (None, a) and there == block]


PLAN = (
    ("take", 0, 0, 0, 0), ("take", 0, 1, 0, 0), ("take", 0, 0, 1, 0), ("take", 0, 0, 7, 0), ("ready", 4, 5),
    ("ready", 5, 8), ("take", 0, 0, 0, 1), ("ready", 8, 24), ("take", 0, 1, 1, 0), ("take", 0, 1, 7, 0),
    ("take", 0, 1, 0, 1), ("take", 0, 0, 2, 0), ("take", 0, 0, 6, 0), ("take", 0, 0, 1, 1),
    ("take", 0, 1, 2, 0), ("take", 0, 1, 6, 0), ("take", 0, 0, 7, 1), ("share", 0, 0, 0),
    ("take", 0, 1, 1, 1), ("take", 0, 0, 3, 0), ("take", 0, 0, 5, 0), ("take", 0, 1, 7, 1),
    ("share", 0, 1, 0), ("take", 0, 1, 3, 0), ("take", 0, 1, 5, 0), ("take", 0, 0, 2, 1),
    ("take", 0, 0, 6, 1), ("take", 0, 0, 4, 0), ("share", 0, 0, 1), ("take", 1, 0, 0, 0),
    ("take", 0, 1, 2, 1), ("take", 0, 1, 4, 0), ("sec_a", 0, 0), ("take", 0, 0, 3, 1), ("take", 0, 1, 6, 1),
    ("share", 0, 1, 1), ("take", 1, 1, 0, 0), ("take", 0, 0, 5, 1), ("share", 0, 0, 2), ("take", 0, 0, 4, 1),
    ("share", 0, 0, 3), ("sec_a", 0, 2), ("take", 1, 0, 1, 0), ("take", 1, 0, 7, 0), ("take", 1, 0, 0, 1),
    ("sec_a", 0, 1), ("take", 0, 1, 3, 1), ("take", 0, 1, 5, 1), ("share", 0, 1, 2), ("take", 0, 1, 4, 1),
    ("share", 0, 1, 3), ("sec_b", 0, 0), ("take", 1, 1, 1, 0), ("take", 1, 1, 7, 0), ("take", 1, 1, 0, 1),
    ("take", 1, 0, 2, 0), ("sec_a", 0, 3), ("take", 1, 0, 1, 1), ("take", 1, 0, 6, 0), ("sec_b", 0, 2),
    ("take", 1, 0, 7, 1), ("share", 1, 0, 0), ("take", 1, 1, 2, 0), ("sec_c", 0, 0), ("take", 1, 1, 6, 0),
    ("sec_b", 0, 1), ("take", 1, 0, 3, 0), ("take", 1, 1, 1, 1), ("take", 1, 0, 5, 0), ("take", 1, 0, 2, 1),
    ("take", 1, 1, 7, 1), ("share", 1, 1, 0), ("sec_c", 0, 2), ("take", 1, 0, 6, 1), ("sec_b", 0, 3),
    ("take", 1, 1, 3, 0), ("share", 1, 0, 1), ("take", 1, 1, 5, 0), ("sec_c", 0, 1), ("take", 1, 0, 4, 0),
    ("sec_a", 1, 0), ("decode", 0), ("take", 1, 0, 5, 1), ("sec_c", 0, 3), ("take", 1, 0, 3, 1),
    ("take", 1, 1, 2, 1), ("take", 1, 1, 6, 1), ("share", 1, 0, 2), ("share", 1, 1, 1), ("take", 1, 1, 4, 0),
    ("decode", 2), ("collect", 0, 0), ("collect", 0, 1), ("reduce", 0, 1, 1), ("reduce", 0, 7, 1),
    ("sec_a", 1, 2), ("decode", 1), ("collect", 2, 0), ("collect", 2, 1), ("take", 1, 0, 4, 1),
    ("reduce", 1, 1, 1), ("reduce", 1, 7, 1), ("take", 1, 1, 3, 1), ("take", 1, 1, 5, 1), ("share", 1, 0, 3),
    ("share", 1, 1, 2), ("collect", 1, 0), ("reduce", 0, 3, 1), ("sec_b", 1, 0), ("collect", 1, 1),
    ("reduce", 0, 4, 1), ("reduce", 0, 4, 0), ("reduce", 0, 5, 0), ("sec_a", 1, 1), ("reduce", 0, 0, 1),
    ("reduce", 0, 1, 0), ("reduce", 0, 7, 0), ("take", 1, 1, 4, 1), ("share", 1, 1, 3), ("decode", 3),
    ("reduce", 0, 2, 1), ("reduce", 1, 1, 0), ("reduce", 1, 7, 0), ("sec_a", 1, 3), ("sec_c", 1, 0),
    ("collect", 3, 0), ("sec_b", 1, 2), ("collect", 3, 1), ("reduce", 1, 4, 1), ("reduce", 0, 5, 1),
    ("reduce", 1, 4, 0), ("reduce", 1, 5, 1), ("reduce", 0, 3, 0), ("reduce", 1, 3, 0), ("reduce", 1, 0, 1),
    ("dec_grad", 0), ("sec_b", 1, 1), ("dec_grad", 1), ("dec_grad", 2), ("sec_c", 1, 2), ("reduce", 1, 3, 1),
    ("sec_b", 1, 3), ("reduce", 0, 6, 1), ("reduce", 1, 5, 0), ("reduce", 0, 2, 0), ("dec_grad", 3),
    ("sec_c", 1, 1), ("reduce", 1, 6, 1), ("sec_e", 1, 0), ("reduce", 1, 2, 1), ("sec_c", 1, 3),
    ("reduce", 0, 6, 0), ("sec_e", 1, 2), ("enc_near", 0), ("enc_near", 1), ("reduce", 1, 6, 0),
    ("enc_near", 2), ("enc_near", 3), ("reduce", 1, 2, 0), ("sec_e", 1, 1), ("finish", 0), ("sec_e", 1, 3),
    ("enc_grad", 0), ("enc_grad", 1), ("enc_grad", 2), ("finish", 1), ("enc_grad", 3),
)

def kernel(
    x_hbm, we_hbm, be_hbm, wd_hbm, bd_hbm, act_hbm, up_hbm,
    reb_hbm, ge_hbm, gd_hbm,
    xs, us, we, wd, be, bd, act,
    part, full, own, yin, xout, xin, lat, pre,
    dec, cout, cin, stage, sums_in, part_ge, ge, gd, reb,
    load_sem, store_sem, g_s, g_r, gc_s, gc_r,
    ry_s, ry_r, rx_s, rx_r, ay_s, ay_r, dc_s, dc_r, s_s, s_r,
):
    s = lax.axis_index("section")
    l = lax.axis_index("lat")
    y, xl = s // 2, lax.rem(s, 2)
    xh, z, c = l // 16, lax.rem(l, 16) // 2, lax.rem(l, 2)

    def at_lat(h, zz, cc):
        return h * 16 + zz * 2 + cc

    zdev = {step: (s, at_lat(xh, lax.rem(z + step + 8, 8), c)) for step in (-2, -1, 1, 2)}
    xdev = (s, at_lat(1 - xh, z, c))
    cdev = (s, at_lat(xh, z, 1 - c))
    ypos = [lax.rem(y + k, 4) for k in (1, 2, 3)]
    ydev = [(p * 2 + xl, l) for p in ypos]
    sdev = (y * 2 + 1 - xl, l)

    def remote(src, dst, sems, at, dev):
        return pltpu.make_async_remote_copy(
            src_ref=src, dst_ref=dst, send_sem=sems[0].at[at], recv_sem=sems[1].at[at], device_id=dev,
            device_id_type=MESH,
        )

    loads = [
        pltpu.make_async_copy(hbm.at[pl.ds(a * H, H)], ref.at[pl.ds(row(a, 0, 0, 0), H)], load_sem.at[t, a])
        for t, (hbm, ref) in enumerate(((x_hbm, xs), (up_hbm, us)))
        for a in (0, 1)
    ]
    loads += [
        pltpu.make_async_copy(we_hbm, we, load_sem.at[2, 0]),
        pltpu.make_async_copy(wd_hbm, wd, load_sem.at[2, 1]),
        pltpu.make_async_copy(be_hbm, be, load_sem.at[3, 0]),
        pltpu.make_async_copy(bd_hbm, bd, load_sem.at[3, 1]),
    ]
    score, other = y // 2, lax.rem(y, 2)
    for q in range(4):
        a, group = divmod(q, 2)
        for n in range(4):
            odd, half = divmod(n, 2)
            dist = (1 - other) * (3 - 6 * odd) + other * 4 * odd if group else (other + 1) * (1 - 2 * odd)
            owner = at_lat(lax.rem(xh + half, 2), lax.rem(z + dist + 8, 8), lax.rem(c + score, 2))
            loads.append(
                pltpu.make_async_copy(
                    act_hbm.at[pl.ds(pl.multiple_of(owner * B + a * H, H), H)],
                    act.at[q, pl.ds(n * H, H)], load_sem.at[4 + q, n],
                )
            )
    for copy in loads:
        copy.start()

    barrier = pltpu.get_barrier_semaphore()
    everyone = list(zdev.values()) + [xdev, cdev, sdev] + ydev
    for dev in everyone:
        pl.semaphore_signal(barrier, inc=1, device_id=dev, device_id_type=MESH)
    pl.semaphore_wait(barrier, len(everyone))

    sent = []

    def start(copy):
        copy.start()
        sent.append(copy)

    stores = []

    def store(copy):
        copy.start()
        stores.append(copy)

    def flush():
        for copy in sent:
            copy.wait_send()
        sent.clear()

    tokens = (xs, us)

    def spread(t, a, i):
        _, axis, step, here, there = SPREAD[t][i]
        return remote(
            tokens[t].at[pl.ds(row(a, here[0], 0, here[1]), H)], tokens[t].at[pl.ds(row(a, there[0], 0, there[1]), H)],
            (g_s, g_r), (t, a, i), xdev if axis == "x" else zdev[step],
        )

    def gc(t, a, p):
        d = PAIRS[p][0]
        return remote(
            tokens[t].at[pl.ds(row(a, d, 0, 0), 4 * H)], tokens[t].at[pl.ds(row(a, d, 1, 0), 4 * H)],
            (gc_s, gc_r), (t, a, p), cdev,
        )

    def take(t, a, d, half):
        if (d, half) == (0, 0):
            loads[2 * t + a].wait()
        for i in coming(SPREAD[t], a, (d, half)):
            spread(t, a, i).wait_recv()
        for i in leaving(SPREAD[t], a, (d, half)):
            start(spread(t, a, i))

    def share(t, a, p):
        start(gc(t, a, p))

    result = (lat, pre)

    def ry(t, q, k):
        return remote(
            part.at[t, pl.ds(pl.multiple_of(q * CH + ypos[k] * 64, 64), 64)], yin.at[t, q, k],
            (ry_s, ry_r), (t, q, k,), ydev[k],
        )

    def rx(t, q):
        return remote(xout.at[t, q], xin.at[t, q], (rx_s, rx_r), (t, q), sdev)

    def ay(t, q, k):
        rows = pl.ds(pl.multiple_of(q * CH + y * 64, 64), 64)
        return remote(result[t].at[rows], result[t].at[rows], (ay_s, ay_r), (t, q, k,), ydev[k])

    def sec_a(t, q):
        a, group = divmod(q, 2)
        gc(t, a, 2 * group).wait_recv()
        gc(t, a, 2 * group + 1).wait_recv()
        rows = pl.ds(q * CH, CH)
        if t == 0:
            acc = jnp.dot(xs[rows], we[...], preferred_element_type=F32)
        else:
            acc = lax.dot_general(us[rows], wd[...], (((1,), (1,)), ((), ())), preferred_element_type=F32)
        full[...] = acc
        part[t, rows] = acc.astype(BF16)
        for k in (1, 0, 2):
            start(ry(t, q, k))
        own[t, q] = full[pl.ds(pl.multiple_of(y * 64, 64), 64)]

    def sec_b(t, q):
        for k in range(3):
            ry(t, q, k).wait_recv()
        own[t, q] = (
            own[t, q] + yin[t, q, 0].astype(F32) + yin[t, q, 1].astype(F32) + yin[t, q, 2].astype(F32)
        )
        xout[t, q] = own[t, q].astype(BF16)
        start(rx(t, q))

    def sec_c(t, q):
        rx(t, q).wait_recv()
        total = own[t, q] + xin[t, q].astype(F32)
        if t == 0:
            total = total + be[...]
        value = (act[q].astype(F32) * total).astype(BF16)
        result[t][pl.ds(pl.multiple_of(q * CH + y * 64, 64), 64)] = value
        for k in (1, 0, 2):
            start(ay(t, q, k))

    def sec_e(t, q):
        for k in range(3):
            ay(t, q, k).wait_recv()

    def dc(q, p):
        rows = pl.ds(p * 64, 64)
        return remote(cout.at[q, rows], cin.at[q, rows], (dc_s, dc_r), (q, p), cdev)

    def decode(q):
        sec_e(0, q)

        @pl.loop(0, 4)
        def _(n):
            cols = pl.ds(pl.multiple_of(n * 512, 512), 512)
            both = jnp.dot(lat[pl.ds(q * CH, CH)], wd[:, cols], preferred_element_type=F32)
            dec[q, :, cols] = both[:128]
            cout[q, :, cols] = both[128:].astype(BF16)

        start(dc(q, 0))
        start(dc(q, 1))

    def summed(a, i):
        _, axis, step, _, _ = SUM[i]
        return remote(
            stage.at[a, i], sums_in.at[a, i], (s_s, s_r), (a, i), xdev if axis == "x" else zdev[step]
        )

    def total(a, d, half, cols):
        group, place = divmod(PLACE[d], 4)
        rows = pl.ds(place * 32 + half * H, H)
        value = dec[2 * a + group, rows, cols] + cin[2 * a + group, rows, cols].astype(F32)
        for i in coming(SUM, a, (d, half)):
            value = value + sums_in[a, i, :, cols].astype(F32)
        return value

    def collect(q, p):
        dc(q, p).wait_recv()

    def arrived(a, d, half):
        for i in coming(SUM, a, (d, half)):
            summed(a, i).wait_recv()

    def reduce(a, d, half):
        arrived(a, d, half)
        (i,) = leaving(SUM, a, (d, half))

        @pl.loop(0, 2)
        def _(n):
            cols = pl.ds(pl.multiple_of(n * 1024, 1024), 1024)
            stage[a, i, :, cols] = total(a, d, half, cols).astype(BF16)

        start(summed(a, i))

    def finish(a):
        arrived(a, 0, 0)
        rows = pl.ds(a * H, H)

        @pl.loop(0, 2)
        def _(n):
            cols = pl.ds(pl.multiple_of(n * 1024, 1024), 1024)
            reb[rows, cols] = (total(a, 0, 0, cols) + bd[:, cols]).astype(BF16)

        store(pltpu.make_async_copy(reb.at[rows], reb_hbm.at[rows], store_sem.at[a]))

    def dec_grad(n):
        cols = pl.ds(n * 512, 512)
        gd[:, cols] = lax.dot_general(
            lat[...], us[:, cols], (((0,), (0,)), ((), ())), preferred_element_type=F32
        ).astype(BF16)
        if n == 3:
            store(pltpu.make_async_copy(gd, gd_hbm, store_sem.at[2]))

    def enc_tokens(rows, group):
        value = 0.0
        for q in (group, 2 + group):
            at = pl.ds(q * CH, CH)
            value = value + lax.dot_general(
                xs[at, rows], pre[at], (((0,), (0,)), ((), ())), preferred_element_type=F32
            )
        return value

    def enc_near(n):
        for m in (0, 1):
            rows = pl.ds(n * 512 + m * 256, 256)
            part_ge[rows] = enc_tokens(rows, 0)

    def enc_grad(n):
        for m in (0, 1):
            rows = pl.ds(n * 512 + m * 256, 256)
            ge[rows] = (part_ge[rows] + enc_tokens(rows, 1)).astype(BF16)
        rows = pl.ds(n * 512, 512)
        store(pltpu.make_async_copy(ge.at[rows], ge_hbm.at[rows], store_sem.at[3 + n]))

    def ready(first, last):
        for i in range(first, last):
            loads[i].wait()

    phases = {
        f.__name__: f
        for f in (
            ready, take, share, sec_a, sec_b, sec_c, sec_e, decode, collect, reduce, finish, dec_grad, enc_near,
            enc_grad,
        )
    }
    plan = [(phases[name], args) for name, *args in PLAN]
    for phase, args in plan:
        phase(*args)
    flush()
    for copy in stores:
        copy.wait()


def copy_out(reb, ge, gd, reb_out, ge_out, gd_out, reb_v, ge_v, gd_v, sems):
    pieces = [(reb, reb_v, reb_out, pl.ds(0, B))]
    for src, held, dst in ((ge, ge_v, ge_out), (gd, gd_v, gd_out)):
        step = src.shape[0] // 4
        pieces += [(src, held, dst, pl.ds(n * step, step)) for n in range(4)]
    ins = [
        pltpu.make_async_copy(src.at[rows], held.at[rows], sems.at[0, n])
        for n, (src, held, _, rows) in enumerate(pieces)
    ]
    outs = [
        pltpu.make_async_copy(held.at[rows], dst.at[rows], sems.at[1, n])
        for n, (_, held, dst, rows) in enumerate(pieces)
    ]
    for copy in ins:
        copy.start()
    for arriving, leaving in zip(ins, outs):
        arriving.wait()
        leaving.start()
    for copy in outs:
        copy.wait()


def per_device(stacked, enc_weight, enc_bias, dec_weight, dec_bias, active, upstream):
    hbm = pl.BlockSpec(memory_space=pl.ANY)
    dma = pltpu.SemaphoreType.DMA
    shapes = (
        jax.ShapeDtypeStruct((B, FEAT), BF16),
        jax.ShapeDtypeStruct((FEAT, LATS), BF16),
        jax.ShapeDtypeStruct((LATS, FEAT), BF16),
    )
    outs = pl.pallas_call(
        kernel,
        out_shape=shapes,
        in_specs=[hbm] * 7,
        out_specs=(hbm,) * 3,
        scratch_shapes=[
            pltpu.VMEM((TOK, FEAT), BF16),
            pltpu.VMEM((TOK, FEAT), BF16),
            pltpu.VMEM((FEAT, LATS), BF16),
            pltpu.VMEM((LATS, FEAT), BF16),
            pltpu.VMEM((1, LATS), F32),
            pltpu.VMEM((1, FEAT), F32),
            pltpu.VMEM((4, 64, LATS), jnp.int32),
            pltpu.VMEM((2, TOK, LATS), BF16),
            pltpu.VMEM((CH, LATS), F32),
            pltpu.VMEM((2, 4, 64, LATS), F32),
            pltpu.VMEM((2, 4, 3, 64, LATS), BF16),
            pltpu.VMEM((2, 4, 64, LATS), BF16),
            pltpu.VMEM((2, 4, 64, LATS), BF16),
            pltpu.VMEM((TOK, LATS), BF16),
            pltpu.VMEM((TOK, LATS), BF16),
            pltpu.VMEM((4, 128, FEAT), F32),
            pltpu.VMEM((4, 128, FEAT), BF16),
            pltpu.VMEM((4, 128, FEAT), BF16),
            pltpu.VMEM((2, len(SUM), H, FEAT), BF16),
            pltpu.VMEM((2, len(SUM), H, FEAT), BF16),
            pltpu.VMEM((FEAT, LATS), F32),
            pltpu.VMEM((FEAT, LATS), BF16),
            pltpu.VMEM((LATS, FEAT), BF16),
            pltpu.VMEM((B, FEAT), BF16),
            dma((8, 4)), dma((7,)),
            dma((2, 2, max(map(len, SPREAD)))), dma((2, 2, max(map(len, SPREAD)))), dma((2, 2, 4)), dma((2, 2, 4)),
            dma((2, 4, 3)), dma((2, 4, 3)), dma((2, 4)), dma((2, 4)), dma((2, 4, 3)), dma((2, 4, 3)),
            dma((4, 2)), dma((4, 2)), dma((2, len(SUM))), dma((2, len(SUM))),
        ],
        compiler_params=pltpu.CompilerParams(
            collective_id=0, has_side_effects=True, vmem_limit_bytes=58 << 20
        ),
        cost_estimate=pl.CostEstimate(flops=10 * 1024 * 2048 * 512, bytes_accessed=14 << 20, transcendentals=0),
    )(
        stacked, enc_weight, enc_bias.reshape(1, -1), dec_weight, dec_bias.reshape(1, -1), active, upstream
    )
    return pl.pallas_call(
        copy_out,
        out_shape=shapes,
        in_specs=[hbm] * 3,
        out_specs=(hbm,) * 3,
        scratch_shapes=[
            pltpu.VMEM((B, FEAT), BF16),
            pltpu.VMEM((FEAT, LATS), BF16),
            pltpu.VMEM((LATS, FEAT), BF16),
            dma((2, 9)),
        ],
        compiler_params=pltpu.CompilerParams(vmem_limit_bytes=58 << 20),
        cost_estimate=pl.CostEstimate(flops=0, bytes_accessed=9 << 20, transcendentals=0),
    )(*outs)


def solution(mesh):
    placed = (
        P("lat", "section"),
        P("section", "lat"),
        P("lat"),
        P("lat", "section"),
        P("section"),
        P(None, "lat"),
        P("lat", "section"),
    )
    return jax.shard_map(
        per_device,
        mesh=mesh,
        in_specs=placed,
        out_specs=(P("lat", "section"), P("section", "lat"), P("lat", "section")),
        check_vma=False,
    )
```
